512 devices in a mesh: row: 16 (over x, z_hi, core), col: 8 (over z_lo), depth: 4 (over y).
Axes of the slice: x: 4, y: 4, z: 16 (z_hi: 2, z_lo: 8; z = z_hi * 8 + z_lo), core: 2. Of those that a mesh axis runs over, the one named last changes fastest.
Arguments:
- a_blocks: float32 [16, 8, 4, 4, 128, 128], P('row', 'col', 'depth'), may hold values from -0.5 to 0.5
- b_blocks: float32 [16, 8, 4, 4, 128, 128], P('row', 'col', 'depth'), may hold values from -1 to 1
- triples: int32 [16, 8, 4, 16, 16, 3], P('row', 'col', 'depth'), may hold values from 0 to 31, as said below
- live: int32 [16, 8, 4, 16], P('row', 'col', 'depth'), may hold values from 1 to 16, as said below
- c_order: int32 [16, 8, 16], P('row', 'col'), may hold values from 0 to 15, as said below
Outputs:
- c_blocks: float32 [16, 8, 4, 4, 128, 128], P('row', 'col', 'depth')
The draws below stay inside these ranges and needn't reach their ends.
Inputs may be any that keep to these rules, and one draw needn't show every extreme that they name: `triples`: in each triple the first entry is below 32, the second below 4, the third below 16. `live`: loads differ strongly between devices. For each grid position (r, c), c_order[r, c] names each of its 16 product slots exactly once; different grid positions have independent orders.
All inputs are finite; a program needn't handle non-finite values.
Results may differ from the reference program's by a relative error of at most 0.0003.
Values sent between devices are 32-bit elements; how exact they have to be, the bound alone decides.
A program may use at most 64 MiB of HBM per device.

```python
import jax
import jax.numpy as jnp
from jax import lax

BS = 128
ASL = 4
BSL = 4
CSL = 16
TCAP = 16
COUT = 4
N_ROW = 16
N_COL = 8
N_DEPTH = 4


def draw_triples(key, part):
    key = jax.random.fold_in(key, 11)
    key_list = jax.random.split(key, 3)
    grid_shape = (N_ROW, N_COL, N_DEPTH, N_ROW, TCAP)
    first_ids = jax.random.randint(key_list[0], grid_shape, 0, ASL * N_COL)
    second_ids = jax.random.randint(key_list[1], grid_shape, 0, BSL)
    third_ids = jax.random.randint(key_list[2], grid_shape, 0, CSL)
    return jnp.stack([first_ids, second_ids, third_ids], axis=-1).astype(jnp.int32)


def draw_live(key, part):
    key = jax.random.fold_in(key, 23)
    key_list = jax.random.split(key, 4)
    grid_shape = (N_ROW, N_COL, N_DEPTH, N_ROW)
    light_load = jax.random.randint(key_list[0], grid_shape, 1, TCAP // 2 + 1)
    heavy_load = jax.random.randint(key_list[1], grid_shape, TCAP // 2, TCAP + 1)
    loaded = jax.random.randint(key_list[2], (N_ROW, N_COL, N_DEPTH, 1), 0, 4) == 0
    counts = jnp.where(loaded, heavy_load, light_load)
    entries = N_ROW * N_COL * N_DEPTH * N_ROW
    flat_ids = jnp.arange(entries, dtype=jnp.int32).reshape(grid_shape)
    chosen = jax.random.randint(key_list[3], (), 0, entries)
    return jnp.where(flat_ids == chosen, TCAP, counts).astype(jnp.int32)


def draw_c_order(key, part):
    key = jax.random.fold_in(key, 37)
    key_list = jax.random.split(key, N_ROW * N_COL)
    base_order = jnp.arange(CSL, dtype=jnp.int32)
    orders = jax.vmap(lambda sub_key: jax.random.permutation(sub_key, base_order))(key_list)
    return orders.reshape(N_ROW, N_COL, CSL).astype(jnp.int32)


def shard_levels(stream_key, shape, pieces, smallest, high):
    def one(position, shards_of):
        draws = jax.random.uniform(jax.random.fold_in(jax.random.fold_in(stream_key, 6), position), (shards_of,), jnp.float32, smallest / len(pieces), high / len(pieces))
        return jnp.repeat(jnp.exp(draws), shape[position] // shards_of).reshape((-1,) + (1,) * (len(shape) - position - 1))

    level = one(*pieces[0])
    for cut in pieces[1:]:
        level = level * one(*cut)
    return level


def normal_values(key, extent, spread, most, cuts=(), held_as=jnp.bfloat16):
    factor_of = shard_levels(key, extent, cuts, -0.22, 0.18) if cuts else 1.0
    result = jax.random.normal(key, extent, jnp.float32) * spread * factor_of
    return jnp.minimum(jnp.maximum(result, -most), most).astype(held_as)


def setup_inputs(seed: int = 0) -> dict:
    splits = jax.random.split(jax.random.key(seed), 6)
    a_blocks = normal_values(splits[0], (N_ROW, N_COL, N_DEPTH, ASL, BS, BS), BS ** -0.5, 0.5, ((0, 16), (1, 8), (2, 4)), jnp.float32)
    b_blocks = normal_values(splits[1], (N_ROW, N_COL, N_DEPTH, BSL, BS, BS), 0.125, 1.0, ((0, 16), (1, 8), (2, 4)), jnp.float32)
    triples = draw_triples(jax.random.fold_in(splits[5], 71), 0)
    live = draw_live(jax.random.fold_in(splits[5], 71), 0)
    c_order = draw_c_order(jax.random.fold_in(splits[5], 71), 0)
    return dict(a_blocks=a_blocks, b_blocks=b_blocks, triples=triples, live=live, c_order=c_order)


def block_products(a_panel, b_shard, triple_rows, live_count, running):
    width = triple_rows.shape[0]
    left_blocks = jnp.take(a_panel, triple_rows[:, 0], axis=0)
    right_blocks = jnp.take(b_shard, triple_rows[:, 1], axis=0)
    products = jnp.einsum("tik,tkj->tij", left_blocks, right_blocks, precision=lax.Precision.HIGHEST)
    active_mask = (jnp.arange(width, dtype=jnp.int32) < live_count).astype(jnp.float32)
    slot_ids = jnp.arange(running.shape[0], dtype=jnp.int32)
    placing = (triple_rows[:, 2][None, :] == slot_ids[:, None]).astype(jnp.float32) * active_mask[None, :]
    return running + jnp.einsum("ct,tij->cij", placing, products, precision=lax.Precision.HIGHEST)


def reference(a_blocks, b_blocks, triples, live, c_order):
    def panel_total(flat_index):
        grid_row = flat_index // N_COL
        grid_col = flat_index % N_COL

        def depth_term(depth_pos, summed):
            a_panel = a_blocks[grid_row, :, depth_pos].reshape(-1, BS, BS)
            b_panel = b_blocks[:, grid_col, depth_pos]
            triple_table = triples[grid_row, grid_col, depth_pos]
            live_table = live[grid_row, grid_col, depth_pos]

            def one_step(step_index, running):
                return block_products(a_panel, b_panel[step_index], triple_table[step_index], live_table[step_index], running)

            return lax.fori_loop(0, N_ROW, one_step, summed)

        summed = lax.fori_loop(0, N_DEPTH, depth_term, jnp.zeros((CSL, BS, BS), jnp.float32))
        slot_order = c_order[grid_row, grid_col]
        return jnp.take(summed, slot_order, axis=0).reshape(N_DEPTH, COUT, BS, BS)

    stacked = lax.map(panel_total, jnp.arange(N_ROW * N_COL, dtype=jnp.int32))
    return stacked.reshape(N_ROW, N_COL, N_DEPTH, COUT, BS, BS)
```

```python
import functools

import jax
import jax.numpy as jnp
from jax import lax
from jax.experimental import pallas as pl
from jax.experimental.pallas import tpu as pltpu
from jax.sharding import PartitionSpec as P

MESH = pl.DeviceIdType.MESH
NX, NY, NZ, NC = 4, 4, 16, 8
STEPS, TCAP, SLOTS, OWN = 16, 16, 16, 4
HA, HB = 2, 4
B_START = (2, 4)


def split_pair(block):
    high = block.astype(jnp.bfloat16)
    low = (block - high.astype(jnp.float32)).astype(jnp.bfloat16)
    return jnp.concatenate([high, low], axis=-1)


def kernel(
    a_ref, b_ref, trip, live, order, out,
    abuf, bbuf, ahl, bhl, cum, sbuf, rbuf, prev, last,
    ss_a, rs_a, ss_x0, rs_x0, ss_k0, rs_k0, ss_z, rs_z, ss_x1, rs_x1, ss_k1, rs_k1, ss_c, rs_c,
):
    row, c, y = lax.axis_index("row"), lax.axis_index("col"), lax.axis_index("depth")
    x, zh, k = row // 4, (row // 2) % 2, row % 2

    def dev(dx=0, dz=0, dk=0, dc=0, dy=0):
        r = ((x + dx + NX) % NX) * 4 + ((zh + dz) % 2) * 2 + (k + dk) % 2
        return (r, c + dc, (y + dy + NY) % NY)

    def copy(src, dst, ss, rs, to):
        return pltpu.make_async_remote_copy(
            src_ref=src, dst_ref=dst, send_sem=ss, recv_sem=rs, device_id=to, device_id_type=MESH
        )

    barrier = pltpu.get_barrier_semaphore()
    partners = [dev(dx=1), dev(dx=2), dev(dx=3), dev(dz=1), dev(dk=1), dev(dy=1), dev(dy=2), dev(dy=3)]
    for p in partners:
        pl.semaphore_signal(barrier, inc=1, device_id=p, device_id_type=MESH)

    @pl.when(c > 0)
    def _():
        pl.semaphore_signal(barrier, inc=1, device_id=dev(dc=-1), device_id_type=MESH)

    @pl.when(c < NC - 1)
    def _():
        pl.semaphore_signal(barrier, inc=1, device_id=dev(dc=1), device_id_type=MESH)

    ends = (c > 0).astype(jnp.int32) + (c < NC - 1).astype(jnp.int32)
    pl.semaphore_wait(barrier, len(partners) + ends)

    wa = 4 // HA

    def a_copy(direction, t, h):
        j = c - t * direction
        part = pl.ds(h * wa, wa)
        src = a_ref.at[part] if t == 0 else abuf.at[j, part]
        return copy(
            src, abuf.at[j, part], ss_a.at[(1 - direction) // 2, t, h], rs_a.at[j, h], dev(dc=direction)
        )

    def a_arrived(j, h):
        part = pl.ds(h * wa, wa)
        copy(abuf.at[j, part], abuf.at[j, part], ss_a.at[0, 0, h], rs_a.at[j, h], dev(dc=0, dk=1)).wait_recv()

    def x0_copy(d):
        return copy(b_ref, bbuf.at[0, d, 0], ss_x0.at[d - 1], rs_x0.at[d - 1], dev(dx=-d))

    def k0_copy(d):
        src = b_ref if d == 0 else bbuf.at[0, d, 0]
        return copy(src, bbuf.at[0, d, 1], ss_k0.at[d], rs_k0.at[d], dev(dk=1))

    wb = 4 // HB

    def z_copy(h):
        part = pl.ds(h * wb, wb)
        return copy(b_ref.at[part], bbuf.at[1, 0, 0, part], ss_z.at[h], rs_z.at[h], dev(dz=1))

    def x1_copy(d, h):
        part = pl.ds(h * wb, wb)
        return copy(
            bbuf.at[1, 0, 0, part], bbuf.at[1, d, 0, part], ss_x1.at[d - 1, h], rs_x1.at[d - 1, h], dev(dx=-d)
        )

    def k1_copy(d, h):
        part = pl.ds(h * wb, wb)
        return copy(bbuf.at[1, d, 0, part], bbuf.at[1, d, 1, part], ss_k1.at[d, h], rs_k1.at[d, h], dev(dk=1))

    def c_copy(d):
        return copy(sbuf.at[d - 1], rbuf.at[d - 1], ss_c.at[d - 1], rs_c.at[d - 1], dev(dy=d))

    def each_a(t, h, act):
        @pl.when((c - t >= 0) & (c < NC - 1))
        def _():
            act(a_copy(1, t, h))

        @pl.when((c + t <= NC - 1) & (c > 0))
        def _():
            act(a_copy(-1, t, h))

    for h in range(HA):
        each_a(0, h, lambda cp: cp.start())
    for d in (2, 1, 3):
        x0_copy(d).start()
    k0_copy(0).start()

    def start_z(t):
        for core in range(2):
            if B_START[core] == t:
                @pl.when(k == core)
                def _():
                    for h in range(HB):
                        z_copy(h).start()

    start_z(0)

    def step_of(i):
        dz, dx, dk = i // 8, (i // 2) % 4, i % 2
        return ((x + dx) % NX) * 4 + ((zh + dz) % 2) * 2 + (k + dk) % 2

    def chain(i, heads):
        s = step_of(i)
        count = live[s]
        for t in range(TCAP):
            q = trip[s, t, 2]
            before = jnp.int32(STEPS * TCAP)
            for n in range(SLOTS):
                before = jnp.where(q == n, heads[n], before)
            prev[i * TCAP + t] = before
            here = jnp.where(t < count, q, SLOTS)
            heads = tuple(jnp.where(here == n, i * TCAP + t, heads[n]) for n in range(SLOTS))
        return heads

    none = jnp.int32(STEPS * TCAP)
    heads = lax.fori_loop(0, STEPS, chain, (none,) * SLOTS)
    for n in range(SLOTS):
        last[n] = heads[n]
    cum[STEPS * TCAP] = jnp.zeros((128, 128), jnp.float32)

    def split_a(j, src):
        for n in range(4):
            ahl[j * 4 + n] = split_pair(src(n))

    split_a(c, lambda n: a_ref[n])

    def split_b(i, src):
        for n in range(4):
            bhl[i * 4 + n] = split_pair(src(n))

    split_b(0, lambda n: b_ref[n])

    for t in range(1, NC):
        for h in range(HA):
            @pl.when(c - t >= 0)
            def _():
                a_arrived(c - t, h)

            @pl.when(c + t <= NC - 1)
            def _():
                a_arrived(c + t, h)

            each_a(t, h, lambda cp: cp.start())

        start_z(t)

        @pl.when(c - t >= 0)
        def _():
            split_a(c - t, lambda n: abuf[c - t, n])

        @pl.when(c + t <= NC - 1)
        def _():
            split_a(c + t, lambda n: abuf[c + t, n])

        if t <= 3:
            d = (1, 3, 2)[t - 1]
            x0_copy(d).wait_recv()
            k0_copy(d).start()
            split_b(d * 2, lambda n: bbuf[0, d, 0, n])

    def products(i):
        s = step_of(i)

        def one(t, carry):
            left = ahl[trip[s, t, 0]]
            right = bhl[i * 4 + trip[s, t, 1]]
            both = jnp.dot(
                left, jnp.concatenate([right, right], axis=0), preferred_element_type=jnp.float32
            )
            cum[i * TCAP + t] = cum[prev[i * TCAP + t]] + (both[:, :128] + both[:, 128:])
            return carry

        lax.fori_loop(0, TCAP, one, 0, unroll=4)

    for d in range(4):
        k0_copy(d).wait_recv()
        split_b(d * 2 + 1, lambda n: bbuf[0, d, 1, n])

    def group(i, carry):
        products(i)
        return carry

    lax.fori_loop(0, 8, group, 0)

    for h in range(HB):
        z_copy(h).wait_recv()
        for d in (2, 1, 3):
            x1_copy(d, h).start()
        k1_copy(0, h).start()
        for d in (1, 3, 2):
            x1_copy(d, h).wait_recv()
            k1_copy(d, h).start()
    for d in range(4):
        split_b(8 + d * 2, lambda n: bbuf[1, d, 0, n])
    for d in range(4):
        for h in range(HB):
            k1_copy(d, h).wait_recv()
        split_b(8 + d * 2 + 1, lambda n: bbuf[1, d, 1, n])

    lax.fori_loop(8, 16, group, 0)

    for d in (2, 1, 3):
        owner = (y + d) % NY
        for n in range(OWN):
            sbuf[d - 1, n] = cum[last[order[owner * OWN + n]]]
        c_copy(d).start()
    for n in range(OWN):
        out[n] = cum[last[order[y * OWN + n]]]
    for d in (1, 3, 2):
        c_copy(d).wait_recv()
        out[...] += rbuf[d - 1]

    for h in range(HA):
        for t in range(NC):
            each_a(t, h, lambda cp: cp.wait_send())
    for d in range(1, 4):
        x0_copy(d).wait_send()
        c_copy(d).wait_send()
        for h in range(HB):
            x1_copy(d, h).wait_send()
    for h in range(HB):
        z_copy(h).wait_send()
    for d in range(4):
        k0_copy(d).wait_send()
        for h in range(HB):
            k1_copy(d, h).wait_send()


def on_device(a_blocks, b_blocks, triples, live, c_order):
    f32, bf16 = jnp.float32, jnp.bfloat16
    vmem, smem = pl.BlockSpec(memory_space=pltpu.VMEM), pl.BlockSpec(memory_space=pltpu.SMEM)
    dma = pltpu.SemaphoreType.DMA
    result = pl.pallas_call(
        kernel,
        out_shape=jax.ShapeDtypeStruct((OWN, 128, 128), f32),
        in_specs=[vmem, vmem, smem, smem, smem],
        out_specs=vmem,
        scratch_shapes=[
            pltpu.VMEM((NC, 4, 128, 128), f32),
            pltpu.VMEM((2, 4, 2, 4, 128, 128), f32),
            pltpu.VMEM((NC * 4, 128, 256), bf16),
            pltpu.VMEM((STEPS * 4, 128, 256), bf16),
            pltpu.VMEM((STEPS * TCAP + 1, 128, 128), f32),
            pltpu.VMEM((3, OWN, 128, 128), f32),
            pltpu.VMEM((3, OWN, 128, 128), f32),
            pltpu.SMEM((STEPS * TCAP,), jnp.int32),
            pltpu.SMEM((SLOTS,), jnp.int32),
            dma((2, NC, HA)), dma((NC, HA)),
            dma((3,)), dma((3,)), dma((4,)), dma((4,)),
            dma((HB,)), dma((HB,)), dma((3, HB)), dma((3, HB)), dma((4, HB)), dma((4, HB)),
            dma((3,)), dma((3,)),
        ],
        compiler_params=pltpu.CompilerParams(
            collective_id=0, has_side_effects=True, vmem_limit_bytes=56 * 1024 * 1024
        ),
        name="block_sparse_product",
    )(a_blocks[0, 0, 0], b_blocks[0, 0, 0], triples[0, 0, 0], live[0, 0, 0], c_order[0, 0])
    return result.reshape(1, 1, 1, OWN, 128, 128)


def solution(mesh):
    placed = (
        P("row", "col", "depth", None, None, None),
        P("row", "col", "depth", None, None, None),
        P("row", "col", "depth", None, None, None),
        P("row", "col", "depth", None),
        P("row", "col", None),
    )
    return jax.shard_map(
        on_device,
        mesh=mesh,
        in_specs=placed,
        out_specs=P("row", "col", "depth", None, None, None),
        check_vma=False,
    )
```

```python
import functools

import jax
import jax.numpy as jnp
from jax import lax
from jax.experimental import pallas as pl
from jax.experimental.pallas import tpu as pltpu
from jax.sharding import PartitionSpec as P

MESH = pl.DeviceIdType.MESH
NX, NY, NZ, NC = 4, 4, 16, 8
STEPS, TCAP, SLOTS, OWN = 16, 16, 16, 4
HA = 2
WINDOW = 2
UNROLL = 16


def split_pair(block):
    high = block.astype(jnp.bfloat16)
    low = (block - high.astype(jnp.float32)).astype(jnp.bfloat16)
    return jnp.concatenate([high, low], axis=-1)


def kernel(
    a_ref, b_ref, trip, live, order, out,
    abuf, bbuf, ahl, bhl, cum, sbuf, via, rbuf, prev, last,
    ss_a, rs_a, ss_x0, rs_x0, ss_k0, rs_k0, ss_z, rs_z, ss_x1, rs_x1, ss_k1, rs_k1, ss_c, rs_c,
):
    row, c, y = lax.axis_index("row"), lax.axis_index("col"), lax.axis_index("depth")
    x, zh, k = row // 4, (row // 2) % 2, row % 2

    def dev(dx=0, dz=0, dk=0, dc=0, dy=0):
        r = ((x + dx + NX) % NX) * 4 + ((zh + dz) % 2) * 2 + (k + dk) % 2
        return (r, c + dc, (y + dy + NY) % NY)

    def copy(src, dst, ss, rs, to):
        return pltpu.make_async_remote_copy(
            src_ref=src, dst_ref=dst, send_sem=ss, recv_sem=rs, device_id=to, device_id_type=MESH
        )

    barrier = pltpu.get_barrier_semaphore()
    partners = [dev(dx=1), dev(dx=2), dev(dx=3), dev(dz=1), dev(dk=1), dev(dy=1), dev(dy=-1)]
    for p in partners:
        pl.semaphore_signal(barrier, inc=1, device_id=p, device_id_type=MESH)

    @pl.when(c > 0)
    def _():
        pl.semaphore_signal(barrier, inc=1, device_id=dev(dc=-1), device_id_type=MESH)

    @pl.when(c < NC - 1)
    def _():
        pl.semaphore_signal(barrier, inc=1, device_id=dev(dc=1), device_id_type=MESH)

    ends = (c > 0).astype(jnp.int32) + (c < NC - 1).astype(jnp.int32)
    pl.semaphore_wait(barrier, len(partners) + ends)

    wa = 4 // HA

    def a_copy(direction, t, h):
        j = c - t * direction
        part = pl.ds(h * wa, wa)
        src = a_ref.at[part] if t == 0 else abuf.at[j, part]
        return copy(
            src, abuf.at[j, part], ss_a.at[(1 - direction) // 2, t, h], rs_a.at[j, h], dev(dc=direction)
        )

    def a_arrived(j, h):
        part = pl.ds(h * wa, wa)
        copy(abuf.at[j, part], abuf.at[j, part], ss_a.at[0, 0, h], rs_a.at[j, h], dev(dc=0, dk=1)).wait_recv()

    def x0_copy(d):
        return copy(b_ref, bbuf.at[0, d, 0], ss_x0.at[d - 1], rs_x0.at[d - 1], dev(dx=-d))

    def k0_copy(d):
        src = b_ref if d == 0 else bbuf.at[0, d, 0]
        return copy(src, bbuf.at[0, d, 1], ss_k0.at[d], rs_k0.at[d], dev(dk=1))

    def z_copy():
        return copy(b_ref, bbuf.at[1, 0, 0], ss_z.at[0], rs_z.at[0], dev(dz=1))

    def x1_copy(d):
        return copy(bbuf.at[1, 0, 0], bbuf.at[1, d, 0], ss_x1.at[d - 1], rs_x1.at[d - 1], dev(dx=-d))

    def k1_copy(d):
        return copy(bbuf.at[1, d, 0], bbuf.at[1, d, 1], ss_k1.at[d], rs_k1.at[d], dev(dk=1))

    def c_copy(side, stage):
        keep = pl.ds(2 * (side if stage == 2 else 1 - side), 2)
        dst = via.at[side] if stage == 0 else rbuf.at[side, keep]
        return copy(
            sbuf.at[side, stage], dst, ss_c.at[side, stage], rs_c.at[side, stage], dev(dy=1 - 2 * side)
        )

    def each_a(n, act, done=False):
        t, h = divmod(n, HA)
        last_of = (n + WINDOW) // HA
        right, left = (c - t >= 0) & (c < NC - 1), (c + t <= NC - 1) & (c > 0)
        if done:
            right, left = right & (c - last_of < 0), left & (c + last_of > NC - 1)

        @pl.when(right)
        def _():
            act(a_copy(1, t, h))

        @pl.when(left)
        def _():
            act(a_copy(-1, t, h))

    def send_a(n):
        t, h = divmod(n, HA)
        if n >= WINDOW:
            to, ho = divmod(n - WINDOW, HA)

            @pl.when((c - t >= 0) & (c < NC - 1))
            def _():
                a_copy(1, to, ho).wait_send()

            @pl.when((c + t <= NC - 1) & (c > 0))
            def _():
                a_copy(-1, to, ho).wait_send()
        each_a(n, lambda cp: cp.start())

    z_copy().start()
    for h in range(HA):
        send_a(h)
    for d in (2, 1, 3):
        x0_copy(d).start()
    k0_copy(0).start()

    def step_of(i):
        dz, dx, dk = i // 8, (i // 2) % 4, i % 2
        return ((x + dx) % NX) * 4 + ((zh + dz) % 2) * 2 + (k + dk) % 2

    def chain(i, heads):
        s = step_of(i)
        count = live[s]
        for t in range(TCAP):
            q = trip[2, s, t]
            before = jnp.int32(STEPS * TCAP)
            for n in range(SLOTS):
                before = jnp.where(q == n, heads[n], before)
            prev[i * TCAP + t] = before
            here = jnp.where(t < count, q, SLOTS)
            heads = tuple(jnp.where(here == n, i * TCAP + t, heads[n]) for n in range(SLOTS))
        return heads

    none = jnp.int32(STEPS * TCAP)
    heads = lax.fori_loop(0, STEPS, chain, (none,) * SLOTS)
    for n in range(SLOTS):
        last[n] = heads[n]
    cum[STEPS * TCAP] = jnp.zeros((128, 128), jnp.float32)

    def split_a(j, src):
        for n in range(4):
            ahl[j * 4 + n] = split_pair(src(n))

    split_a(c, lambda n: a_ref[n])

    def split_b(i, src):
        for n in range(4):
            bhl[i * 4 + n] = split_pair(src(n))

    split_b(0, lambda n: b_ref[n])

    z_copy().wait_recv()
    for d in (2, 1, 3):
        x1_copy(d).start()
    k1_copy(0).start()
    split_b(8, lambda n: bbuf[1, 0, 0, n])

    for t in range(1, NC):
        for h in range(HA):
            @pl.when(c - t >= 0)
            def _():
                a_arrived(c - t, h)

            @pl.when(c + t <= NC - 1)
            def _():
                a_arrived(c + t, h)

            send_a(t * HA + h)

        @pl.when(c - t >= 0)
        def _():
            split_a(c - t, lambda n: abuf[c - t, n])

        @pl.when(c + t <= NC - 1)
        def _():
            split_a(c + t, lambda n: abuf[c + t, n])

        if t <= 3:
            d = (1, 3, 2)[t - 1]
            x0_copy(d).wait_recv()
            k0_copy(d).start()
            split_b(d * 2, lambda n: bbuf[0, d, 0, n])
        if 2 <= t <= 4:
            d = (1, 3, 2)[t - 2]
            x1_copy(d).wait_recv()
            k1_copy(d).start()
            split_b(8 + d * 2, lambda n: bbuf[1, d, 0, n])
        if 4 <= t:
            d = t - 4
            k0_copy(d).wait_recv()
            split_b(d * 2 + 1, lambda n: bbuf[0, d, 1, n])
            k1_copy(d).wait_recv()
            split_b(8 + d * 2 + 1, lambda n: bbuf[1, d, 1, n])

    def products(i, carry):
        s = step_of(i)

        def one(t, carry):
            left = ahl[trip[0, s, t]]
            right = bhl[i * 4 + trip[1, s, t]]
            both = jnp.dot(
                left, jnp.concatenate([right, right], axis=0), preferred_element_type=jnp.float32
            )
            cum[i * TCAP + t] = cum[prev[i * TCAP + t]] + (both[:, :128] + both[:, 128:])
            return carry

        return lax.fori_loop(0, TCAP, one, carry, unroll=UNROLL)

    lax.fori_loop(0, STEPS, products, 0)

    def total(owner, n):
        return cum[last[order[((y + owner + NY) % NY) * OWN + n]]]

    for stage in (0, 1):
        for side in (0, 1):
            for n in range(2):
                if stage == 0:
                    sbuf[side, 0, n] = total(2, 2 * side + n)
                else:
                    sbuf[side, 1, n] = total(1 - 2 * side, 2 * (1 - side) + n)
            c_copy(side, stage).start()
    for side in (0, 1):
        for n in range(2):
            sbuf[side, 2, n] = total(1 - 2 * side, 2 * side + n)
    for n in range(OWN):
        out[n] = total(0, n)
    for side in (0, 1):
        c_copy(side, 0).wait_recv()
        sbuf[side, 2] += via[side]
        c_copy(side, 2).start()
    for stage in (1, 2):
        for side in (0, 1):
            c_copy(side, stage).wait_recv()
            keep = pl.ds(2 * (side if stage == 2 else 1 - side), 2)
            out[keep] += rbuf[side, keep]

    for n in range(NC * HA):
        each_a(n, lambda cp: cp.wait_send(), done=True)
    z_copy().wait_send()
    for d in range(1, 4):
        x0_copy(d).wait_send()
        x1_copy(d).wait_send()
    for d in range(4):
        k0_copy(d).wait_send()
        k1_copy(d).wait_send()
    for side in (0, 1):
        for stage in range(3):
            c_copy(side, stage).wait_send()


def on_device(a_blocks, b_blocks, triples, live, c_order):
    f32, bf16 = jnp.float32, jnp.bfloat16
    vmem, smem = pl.BlockSpec(memory_space=pltpu.VMEM), pl.BlockSpec(memory_space=pltpu.SMEM)
    dma = pltpu.SemaphoreType.DMA
    result = pl.pallas_call(
        kernel,
        out_shape=jax.ShapeDtypeStruct((OWN, 128, 128), f32),
        in_specs=[vmem, vmem, smem, smem, smem],
        out_specs=vmem,
        scratch_shapes=[
            pltpu.VMEM((NC, 4, 128, 128), f32),
            pltpu.VMEM((2, 4, 2, 4, 128, 128), f32),
            pltpu.VMEM((NC * 4, 128, 256), bf16),
            pltpu.VMEM((STEPS * 4, 128, 256), bf16),
            pltpu.VMEM((STEPS * TCAP + 1, 128, 128), f32),
            pltpu.VMEM((2, 3, 2, 128, 128), f32),
            pltpu.VMEM((2, 2, 128, 128), f32),
            pltpu.VMEM((2, OWN, 128, 128), f32),
            pltpu.SMEM((STEPS * TCAP,), jnp.int32),
            pltpu.SMEM((SLOTS,), jnp.int32),
            dma((2, NC, HA)), dma((NC, HA)),
            dma((3,)), dma((3,)), dma((4,)), dma((4,)),
            dma((1,)), dma((1,)), dma((3,)), dma((3,)), dma((4,)), dma((4,)),
            dma((2, 3)), dma((2, 3)),
        ],
        compiler_params=pltpu.CompilerParams(
            collective_id=0, has_side_effects=True, vmem_limit_bytes=56 * 1024 * 1024
        ),
        name="block_sparse_product",
    )(a_blocks[0, 0, 0], b_blocks[0, 0, 0], jnp.transpose(triples[0, 0, 0], (2, 0, 1)), live[0, 0, 0], c_order[0, 0])
    return result.reshape(1, 1, 1, OWN, 128, 128)


def solution(mesh):
    placed = (
        P("row", "col", "depth", None, None, None),
        P("row", "col", "depth", None, None, None),
        P("row", "col", "depth", None, None, None),
        P("row", "col", "depth", None),
        P("row", "col", None),
    )
    return jax.shard_map(
        on_device,
        mesh=mesh,
        in_specs=placed,
        out_specs=P("row", "col", "depth", None, None, None),
        check_vma=False,
    )
```

```python
import functools

import jax
import jax.numpy as jnp
from jax import lax
from jax.experimental import pallas as pl
from jax.experimental.pallas import tpu as pltpu
from jax.sharding import PartitionSpec as P

MESH = pl.DeviceIdType.MESH
NX, NY, NZ, NC = 4, 4, 16, 8
STEPS, TCAP, SLOTS, BSL, OWN = 16, 16, 16, 4, 4
HA = 2
WINDOW = 2
UNROLL = 64


def split_pair(block):
    high = block.astype(jnp.bfloat16)
    low = (block - high.astype(jnp.float32)).astype(jnp.bfloat16)
    return jnp.concatenate([high, low], axis=-1)


def kernel(
    a_ref, b_ref, trip, live, order, out,
    abuf, bbuf, ahl, bhl, cum, sbuf, via, rbuf, prev, lefts, rights, last,
    ss_a, rs_a, ss_x0, rs_x0, ss_k0, rs_k0, ss_z, rs_z, ss_x1, rs_x1, ss_k1, rs_k1, ss_c, rs_c,
):
    row, c, y = lax.axis_index("row"), lax.axis_index("col"), lax.axis_index("depth")
    x, zh, k = row // 4, (row // 2) % 2, row % 2

    def dev(dx=0, dz=0, dk=0, dc=0, dy=0):
        r = ((x + dx + NX) % NX) * 4 + ((zh + dz) % 2) * 2 + (k + dk) % 2
        return (r, c + dc, (y + dy + NY) % NY)

    def copy(src, dst, ss, rs, to):
        return pltpu.make_async_remote_copy(
            src_ref=src, dst_ref=dst, send_sem=ss, recv_sem=rs, device_id=to, device_id_type=MESH
        )

    barrier = pltpu.get_barrier_semaphore()

    def greet(to):
        pl.semaphore_signal(barrier, inc=1, device_id=to, device_id_type=MESH)

    partners = [dev(dx=1), dev(dx=2), dev(dx=3), dev(dk=1), dev(dy=1), dev(dy=-1)]
    for p in partners:
        greet(p)

    @pl.when(c > 0)
    def _():
        greet(dev(dc=-1))

    @pl.when(c < NC - 1)
    def _():
        greet(dev(dc=1))

    ends = (c > 0).astype(jnp.int32) + (c < NC - 1).astype(jnp.int32)
    pl.semaphore_wait(barrier, len(partners) + ends + zh)
    greet(dev(dz=1))

    wa = 4 // HA

    def a_copy(direction, t, h):
        j = c - t * direction
        part = pl.ds(h * wa, wa)
        src = a_ref.at[part] if t == 0 else abuf.at[j, part]
        return copy(
            src, abuf.at[j, part], ss_a.at[(1 - direction) // 2, t, h], rs_a.at[j, h], dev(dc=direction)
        )

    def a_arrived(j, h):
        part = pl.ds(h * wa, wa)
        copy(abuf.at[j, part], abuf.at[j, part], ss_a.at[0, 0, h], rs_a.at[j, h], dev(dc=0, dk=1)).wait_recv()

    def x0_copy(d):
        return copy(b_ref, bbuf.at[0, d, 0], ss_x0.at[d - 1], rs_x0.at[d - 1], dev(dx=-d))

    def k0_copy(d):
        src = b_ref if d == 0 else bbuf.at[0, d, 0]
        return copy(src, bbuf.at[0, d, 1], ss_k0.at[d], rs_k0.at[d], dev(dk=1))

    def z_copy():
        return copy(b_ref, bbuf.at[1, 0, 0], ss_z.at[0], rs_z.at[0], dev(dz=1))

    def x1_copy(d):
        return copy(bbuf.at[1, 0, 0], bbuf.at[1, d, 0], ss_x1.at[d - 1], rs_x1.at[d - 1], dev(dx=-d))

    def k1_copy(d):
        return copy(bbuf.at[1, d, 0], bbuf.at[1, d, 1], ss_k1.at[d], rs_k1.at[d], dev(dk=1))

    def c_copy(side, stage):
        keep = pl.ds(2 * (side if stage == 2 else 1 - side), 2)
        dst = via.at[side] if stage == 0 else rbuf.at[side, keep]
        return copy(
            sbuf.at[side, stage], dst, ss_c.at[side, stage], rs_c.at[side, stage], dev(dy=1 - 2 * side)
        )

    def each_a(n, act, done=False):
        t, h = divmod(n, HA)
        last_of = (n + WINDOW) // HA
        right, left = (c - t >= 0) & (c < NC - 1), (c + t <= NC - 1) & (c > 0)
        if done:
            right, left = right & (c - last_of < 0), left & (c + last_of > NC - 1)

        @pl.when(right)
        def _():
            act(a_copy(1, t, h))

        @pl.when(left)
        def _():
            act(a_copy(-1, t, h))

    def send_a(n):
        t, h = divmod(n, HA)
        if n >= WINDOW:
            to, ho = divmod(n - WINDOW, HA)

            @pl.when((c - t >= 0) & (c < NC - 1))
            def _():
                a_copy(1, to, ho).wait_send()

            @pl.when((c + t <= NC - 1) & (c > 0))
            def _():
                a_copy(-1, to, ho).wait_send()
        each_a(n, lambda cp: cp.start())

    @pl.when(zh == 1)
    def _():
        z_copy().start()

    for h in range(HA):
        send_a(h)
    for d in (2, 1, 3):
        x0_copy(d).start()
    k0_copy(0).start()

    @pl.when(zh == 0)
    def _():
        pl.semaphore_wait(barrier, 1)
        z_copy().start()

    def step_of(i):
        dz, dx, dk = i // 8, (i // 2) % 4, i % 2
        return ((x + dx) % NX) * 4 + ((zh + dz) % 2) * 2 + (k + dk) % 2

    def chain(i, heads):
        s = step_of(i)
        count = live[s]
        for t in range(TCAP):
            q = trip[2, s, t]
            before = jnp.int32(STEPS * TCAP)
            for n in range(SLOTS):
                before = jnp.where(q == n, heads[n], before)
            prev[i * TCAP + t] = before
            lefts[i * TCAP + t] = trip[0, s, t]
            rights[i * TCAP + t] = i * BSL + trip[1, s, t]
            here = jnp.where(t < count, q, SLOTS)
            heads = tuple(jnp.where(here == n, i * TCAP + t, heads[n]) for n in range(SLOTS))
        return heads

    none = jnp.int32(STEPS * TCAP)
    heads = lax.fori_loop(0, STEPS, chain, (none,) * SLOTS)
    for n in range(SLOTS):
        last[n] = heads[n]
    cum[STEPS * TCAP] = jnp.zeros((128, 128), jnp.float32)

    def split_a(j, src):
        for n in range(4):
            ahl[j * 4 + n] = split_pair(src(n))

    split_a(c, lambda n: a_ref[n])

    def split_b(i, src):
        for n in range(4):
            bhl[i * 4 + n] = split_pair(src(n))

    split_b(0, lambda n: b_ref[n])

    z_copy().wait_recv()
    for d in (2, 1, 3):
        x1_copy(d).start()
    k1_copy(0).start()
    split_b(8, lambda n: bbuf[1, 0, 0, n])

    for t in range(1, NC):
        for h in range(HA):
            @pl.when(c - t >= 0)
            def _():
                a_arrived(c - t, h)

            @pl.when(c + t <= NC - 1)
            def _():
                a_arrived(c + t, h)

            send_a(t * HA + h)

        @pl.when(c - t >= 0)
        def _():
            split_a(c - t, lambda n: abuf[c - t, n])

        @pl.when(c + t <= NC - 1)
        def _():
            split_a(c + t, lambda n: abuf[c + t, n])

        if t <= 3:
            d = (1, 3, 2)[t - 1]
            x0_copy(d).wait_recv()
            k0_copy(d).start()
            split_b(d * 2, lambda n: bbuf[0, d, 0, n])
        if 2 <= t <= 4:
            d = (1, 3, 2)[t - 2]
            x1_copy(d).wait_recv()
            k1_copy(d).start()
            split_b(8 + d * 2, lambda n: bbuf[1, d, 0, n])
        if 4 <= t:
            d = t - 4
            k0_copy(d).wait_recv()
            split_b(d * 2 + 1, lambda n: bbuf[0, d, 1, n])
            k1_copy(d).wait_recv()
            split_b(8 + d * 2 + 1, lambda n: bbuf[1, d, 1, n])

    def product(i, carry):
        right = bhl[rights[i]]
        both = jnp.dot(
            ahl[lefts[i]], jnp.concatenate([right, right], axis=0), preferred_element_type=jnp.float32
        )
        cum[i] = cum[prev[i]] + (both[:, :128] + both[:, 128:])
        return carry

    lax.fori_loop(0, STEPS * TCAP, product, 0, unroll=UNROLL)

    def total(owner, n):
        return cum[last[order[((y + owner + NY) % NY) * OWN + n]]]

    for stage in (0, 1):
        for side in (0, 1):
            for n in range(2):
                if stage == 0:
                    sbuf[side, 0, n] = total(2, 2 * side + n)
                else:
                    sbuf[side, 1, n] = total(1 - 2 * side, 2 * (1 - side) + n)
            c_copy(side, stage).start()
    for side in (0, 1):
        for n in range(2):
            sbuf[side, 2, n] = total(1 - 2 * side, 2 * side + n)
    for n in range(OWN):
        out[n] = total(0, n)
    for side in (0, 1):
        c_copy(side, 0).wait_recv()
        sbuf[side, 2] += via[side]
        c_copy(side, 2).start()
    for stage in (1, 2):
        for side in (0, 1):
            c_copy(side, stage).wait_recv()
            keep = pl.ds(2 * (side if stage == 2 else 1 - side), 2)
            out[keep] += rbuf[side, keep]

    for n in range(NC * HA):
        each_a(n, lambda cp: cp.wait_send(), done=True)
    z_copy().wait_send()
    for d in range(1, 4):
        x0_copy(d).wait_send()
        x1_copy(d).wait_send()
    for d in range(4):
        k0_copy(d).wait_send()
        k1_copy(d).wait_send()
    for side in (0, 1):
        for stage in range(3):
            c_copy(side, stage).wait_send()


def on_device(a_blocks, b_blocks, triples, live, c_order):
    f32, bf16 = jnp.float32, jnp.bfloat16
    vmem, smem = pl.BlockSpec(memory_space=pltpu.VMEM), pl.BlockSpec(memory_space=pltpu.SMEM)
    dma = pltpu.SemaphoreType.DMA
    result = pl.pallas_call(
        kernel,
        out_shape=jax.ShapeDtypeStruct((OWN, 128, 128), f32),
        in_specs=[vmem, vmem, smem, smem, smem],
        out_specs=vmem,
        scratch_shapes=[
            pltpu.VMEM((NC, 4, 128, 128), f32),
            pltpu.VMEM((2, 4, 2, 4, 128, 128), f32),
            pltpu.VMEM((NC * 4, 128, 256), bf16),
            pltpu.VMEM((STEPS * 4, 128, 256), bf16),
            pltpu.VMEM((STEPS * TCAP + 1, 128, 128), f32),
            pltpu.VMEM((2, 3, 2, 128, 128), f32),
            pltpu.VMEM((2, 2, 128, 128), f32),
            pltpu.VMEM((2, OWN, 128, 128), f32),
            pltpu.SMEM((STEPS * TCAP,), jnp.int32),
            pltpu.SMEM((STEPS * TCAP,), jnp.int32),
            pltpu.SMEM((STEPS * TCAP,), jnp.int32),
            pltpu.SMEM((SLOTS,), jnp.int32),
            dma((2, NC, HA)), dma((NC, HA)),
            dma((3,)), dma((3,)), dma((4,)), dma((4,)),
            dma((1,)), dma((1,)), dma((3,)), dma((3,)), dma((4,)), dma((4,)),
            dma((2, 3)), dma((2, 3)),
        ],
        compiler_params=pltpu.CompilerParams(
            collective_id=0, has_side_effects=True, vmem_limit_bytes=56 * 1024 * 1024
        ),
        name="block_sparse_product",
    )(a_blocks[0, 0, 0], b_blocks[0, 0, 0], jnp.transpose(triples[0, 0, 0], (2, 0, 1)), live[0, 0, 0], c_order[0, 0])
    return result.reshape(1, 1, 1, OWN, 128, 128)


def solution(mesh):
    placed = (
        P("row", "col", "depth", None, None, None),
        P("row", "col", "depth", None, None, None),
        P("row", "col", "depth", None, None, None),
        P("row", "col", "depth", None),
        P("row", "col", None),
    )
    return jax.shard_map(
        on_device,
        mesh=mesh,
        in_specs=placed,
        out_specs=P("row", "col", "depth", None, None, None),
        check_vma=False,
    )
```

```python
import functools

import jax
import jax.numpy as jnp
from jax import lax
from jax.experimental import pallas as pl
from jax.experimental.pallas import tpu as pltpu
from jax.sharding import PartitionSpec as P

MESH = pl.DeviceIdType.MESH
NX, NY, NZ, NC = 4, 4, 16, 8
STEPS, TCAP, SLOTS, BSL, OWN = 16, 16, 16, 4, 4
HA = 2
WINDOW = 2
UNROLL = 64
Z_WAIT, FAR_WAIT = 2, 1


def split_pair(block):
    high = block.astype(jnp.bfloat16)
    low = (block - high.astype(jnp.float32)).astype(jnp.bfloat16)
    return jnp.concatenate([high, low], axis=-1)


def kernel(
    a_ref, b_ref, trip, live, order, out,
    abuf, bbuf, ahl, bhl, cum, sbuf, via, rbuf, prev, lefts, rights, last,
    ss_a, rs_a, ss_x0, rs_x0, ss_k0, rs_k0, ss_z, rs_z, ss_x1, rs_x1, ss_k1, rs_k1, ss_c, rs_c,
):
    row, c, y = lax.axis_index("row"), lax.axis_index("col"), lax.axis_index("depth")
    x, zh, k = row // 4, (row // 2) % 2, row % 2

    def dev(dx=0, dz=0, dk=0, dc=0, dy=0):
        r = ((x + dx + NX) % NX) * 4 + ((zh + dz) % 2) * 2 + (k + dk) % 2
        return (r, c + dc, (y + dy + NY) % NY)

    def copy(src, dst, ss, rs, to):
        return pltpu.make_async_remote_copy(
            src_ref=src, dst_ref=dst, send_sem=ss, recv_sem=rs, device_id=to, device_id_type=MESH
        )

    barrier = pltpu.get_barrier_semaphore()

    def greet(to):
        pl.semaphore_signal(barrier, inc=1, device_id=to, device_id_type=MESH)

    partners = [dev(dx=1), dev(dx=2), dev(dx=3), dev(dk=1), dev(dy=1), dev(dy=-1)]
    for p in partners:
        greet(p)

    @pl.when(c > 0)
    def _():
        greet(dev(dc=-1))

    @pl.when(c < NC - 1)
    def _():
        greet(dev(dc=1))

    ends = (c > 0).astype(jnp.int32) + (c < NC - 1).astype(jnp.int32)
    pl.semaphore_wait(barrier, len(partners) + ends + zh)
    greet(dev(dz=1))

    wa = 4 // HA

    def a_copy(direction, t, h):
        j = c - t * direction
        part = pl.ds(h * wa, wa)
        src = a_ref.at[part] if t == 0 else abuf.at[j, part]
        return copy(
            src, abuf.at[j, part], ss_a.at[(1 - direction) // 2, t, h], rs_a.at[j, h], dev(dc=direction)
        )

    def a_arrived(j, h):
        part = pl.ds(h * wa, wa)
        copy(abuf.at[j, part], abuf.at[j, part], ss_a.at[0, 0, h], rs_a.at[j, h], dev(dc=0, dk=1)).wait_recv()

    def x0_copy(d):
        return copy(b_ref, bbuf.at[0, d, 0], ss_x0.at[d - 1], rs_x0.at[d - 1], dev(dx=-d))

    def k0_copy(d):
        src = b_ref if d == 0 else bbuf.at[0, d, 0]
        return copy(src, bbuf.at[0, d, 1], ss_k0.at[d], rs_k0.at[d], dev(dk=1))

    def z_copy():
        return copy(b_ref, bbuf.at[1, 0, 0], ss_z.at[0], rs_z.at[0], dev(dz=1))

    def x1_copy(d):
        return copy(bbuf.at[1, 0, 0], bbuf.at[1, d, 0], ss_x1.at[d - 1], rs_x1.at[d - 1], dev(dx=-d))

    def k1_copy(d):
        return copy(bbuf.at[1, d, 0], bbuf.at[1, d, 1], ss_k1.at[d], rs_k1.at[d], dev(dk=1))

    def c_copy(side, stage):
        keep = pl.ds(2 * (side if stage == 2 else 1 - side), 2)
        dst = via.at[side] if stage == 0 else rbuf.at[side, keep]
        return copy(
            sbuf.at[side, stage], dst, ss_c.at[side, stage], rs_c.at[side, stage], dev(dy=1 - 2 * side)
        )

    def each_a(n, act, done=False):
        t, h = divmod(n, HA)
        last_of = (n + WINDOW) // HA
        right, left = (c - t >= 0) & (c < NC - 1), (c + t <= NC - 1) & (c > 0)
        if done:
            right, left = right & (c - last_of < 0), left & (c + last_of > NC - 1)

        @pl.when(right)
        def _():
            act(a_copy(1, t, h))

        @pl.when(left)
        def _():
            act(a_copy(-1, t, h))

    def send_a(n):
        t, h = divmod(n, HA)
        if n >= WINDOW:
            to, ho = divmod(n - WINDOW, HA)

            @pl.when((c - t >= 0) & (c < NC - 1))
            def _():
                a_copy(1, to, ho).wait_send()

            @pl.when((c + t <= NC - 1) & (c > 0))
            def _():
                a_copy(-1, to, ho).wait_send()
        each_a(n, lambda cp: cp.start())

    for h in range(HA):
        send_a(h)

    @pl.when(zh == 1)
    def _():
        z_copy().start()
    for d in (2, 1, 3):
        x0_copy(d).start()
    k0_copy(0).start()

    def hear_far():
        @pl.when(zh == 0)
        def _():
            pl.semaphore_wait(barrier, 1)
            z_copy().start()

    def step_of(i):
        dz, dx, dk = i // 8, (i // 2) % 4, i % 2
        return ((x + dx) % NX) * 4 + ((zh + dz) % 2) * 2 + (k + dk) % 2

    def chain(i, heads):
        s = step_of(i)
        count = live[s]
        for t in range(TCAP):
            q = trip[2, s, t]
            before = jnp.int32(STEPS * TCAP)
            for n in range(SLOTS):
                before = jnp.where(q == n, heads[n], before)
            prev[i * TCAP + t] = before
            lefts[i * TCAP + t] = trip[0, s, t]
            rights[i * TCAP + t] = i * BSL + trip[1, s, t]
            here = jnp.where(t < count, q, SLOTS)
            heads = tuple(jnp.where(here == n, i * TCAP + t, heads[n]) for n in range(SLOTS))
        return heads

    none = jnp.int32(STEPS * TCAP)
    heads = lax.fori_loop(0, STEPS, chain, (none,) * SLOTS)
    for n in range(SLOTS):
        last[n] = heads[n]
    cum[STEPS * TCAP] = jnp.zeros((128, 128), jnp.float32)

    def split_a(j, src):
        for n in range(4):
            ahl[j * 4 + n] = split_pair(src(n))

    split_a(c, lambda n: a_ref[n])

    def split_b(i, src):
        for n in range(4):
            bhl[i * 4 + n] = split_pair(src(n))

    split_b(0, lambda n: b_ref[n])

    def forward_z():
        z_copy().wait_recv()
        for d in (2, 1, 3):
            x1_copy(d).start()
        k1_copy(0).start()
        split_b(8, lambda n: bbuf[1, 0, 0, n])

    def forward_x0(d):
        x0_copy(d).wait_recv()
        k0_copy(d).start()
        split_b(d * 2, lambda n: bbuf[0, d, 0, n])

    def forward_x1(d):
        x1_copy(d).wait_recv()
        k1_copy(d).start()
        split_b(8 + d * 2, lambda n: bbuf[1, d, 0, n])

    def take_k0(d):
        k0_copy(d).wait_recv()
        split_b(d * 2 + 1, lambda n: bbuf[0, d, 1, n])

    def take_k1(d):
        k1_copy(d).wait_recv()
        split_b(8 + d * 2 + 1, lambda n: bbuf[1, d, 1, n])

    jobs = {t: [] for t in range(NC + 3)}
    jobs[Z_WAIT].append(forward_z)
    for n, d in enumerate((1, 3, 2)):
        jobs[1 + n].append(functools.partial(forward_x0, d))
        jobs[Z_WAIT + 2 + n].append(functools.partial(forward_x1, d))
    for n, d in enumerate((0, 1, 3, 2)):
        jobs[4 + n].append(functools.partial(take_k0, d))
        jobs[Z_WAIT + 3 + n].append(functools.partial(take_k1, d))

    for t in range(1, NC):
        for h in range(HA):
            @pl.when(c - t >= 0)
            def _():
                a_arrived(c - t, h)

            @pl.when(c + t <= NC - 1)
            def _():
                a_arrived(c + t, h)

            send_a(t * HA + h)

        @pl.when(c - t >= 0)
        def _():
            split_a(c - t, lambda n: abuf[c - t, n])

        @pl.when(c + t <= NC - 1)
        def _():
            split_a(c + t, lambda n: abuf[c + t, n])

        if t == FAR_WAIT:
            hear_far()
        for job in jobs[t]:
            job()
    for t in range(NC, NC + 3):
        for job in jobs[t]:
            job()

    def product(i, carry):
        right = bhl[rights[i]]
        both = jnp.dot(
            ahl[lefts[i]], jnp.concatenate([right, right], axis=0), preferred_element_type=jnp.float32
        )
        cum[i] = cum[prev[i]] + (both[:, :128] + both[:, 128:])
        return carry

    lax.fori_loop(0, STEPS * TCAP, product, 0, unroll=UNROLL)

    def total(owner, n):
        return cum[last[order[((y + owner + NY) % NY) * OWN + n]]]

    for stage in (0, 1):
        for side in (0, 1):
            for n in range(2):
                if stage == 0:
                    sbuf[side, 0, n] = total(2, 2 * side + n)
                else:
                    sbuf[side, 1, n] = total(1 - 2 * side, 2 * (1 - side) + n)
            c_copy(side, stage).start()
    for side in (0, 1):
        for n in range(2):
            sbuf[side, 2, n] = total(1 - 2 * side, 2 * side + n)
    for n in range(OWN):
        out[n] = total(0, n)
    for side in (0, 1):
        c_copy(side, 0).wait_recv()
        sbuf[side, 2] += via[side]
        c_copy(side, 2).start()
    for stage in (1, 2):
        for side in (0, 1):
            c_copy(side, stage).wait_recv()
            keep = pl.ds(2 * (side if stage == 2 else 1 - side), 2)
            out[keep] += rbuf[side, keep]

    for n in range(NC * HA):
        each_a(n, lambda cp: cp.wait_send(), done=True)
    z_copy().wait_send()
    for d in range(1, 4):
        x0_copy(d).wait_send()
        x1_copy(d).wait_send()
    for d in range(4):
        k0_copy(d).wait_send()
        k1_copy(d).wait_send()
    for side in (0, 1):
        for stage in range(3):
            c_copy(side, stage).wait_send()


def on_device(a_blocks, b_blocks, triples, live, c_order):
    f32, bf16 = jnp.float32, jnp.bfloat16
    vmem, smem = pl.BlockSpec(memory_space=pltpu.VMEM), pl.BlockSpec(memory_space=pltpu.SMEM)
    dma = pltpu.SemaphoreType.DMA
    result = pl.pallas_call(
        kernel,
        out_shape=jax.ShapeDtypeStruct((OWN, 128, 128), f32),
        in_specs=[vmem, vmem, smem, smem, smem],
        out_specs=vmem,
        scratch_shapes=[
            pltpu.VMEM((NC, 4, 128, 128), f32),
            pltpu.VMEM((2, 4, 2, 4, 128, 128), f32),
            pltpu.VMEM((NC * 4, 128, 256), bf16),
            pltpu.VMEM((STEPS * 4, 128, 256), bf16),
            pltpu.VMEM((STEPS * TCAP + 1, 128, 128), f32),
            pltpu.VMEM((2, 3, 2, 128, 128), f32),
            pltpu.VMEM((2, 2, 128, 128), f32),
            pltpu.VMEM((2, OWN, 128, 128), f32),
            pltpu.SMEM((STEPS * TCAP,), jnp.int32),
            pltpu.SMEM((STEPS * TCAP,), jnp.int32),
            pltpu.SMEM((STEPS * TCAP,), jnp.int32),
            pltpu.SMEM((SLOTS,), jnp.int32),
            dma((2, NC, HA)), dma((NC, HA)),
            dma((3,)), dma((3,)), dma((4,)), dma((4,)),
            dma((1,)), dma((1,)), dma((3,)), dma((3,)), dma((4,)), dma((4,)),
            dma((2, 3)), dma((2, 3)),
        ],
        compiler_params=pltpu.CompilerParams(
            collective_id=0, has_side_effects=True, vmem_limit_bytes=56 * 1024 * 1024
        ),
        name="block_sparse_product",
    )(a_blocks[0, 0, 0], b_blocks[0, 0, 0], jnp.transpose(triples[0, 0, 0], (2, 0, 1)), live[0, 0, 0], c_order[0, 0])
    return result.reshape(1, 1, 1, OWN, 128, 128)


def solution(mesh):
    placed = (
        P("row", "col", "depth", None, None, None),
        P("row", "col", "depth", None, None, None),
        P("row", "col", "depth", None, None, None),
        P("row", "col", "depth", None),
        P("row", "col", None),
    )
    return jax.shard_map(
        on_device,
        mesh=mesh,
        in_specs=placed,
        out_specs=P("row", "col", "depth", None, None, None),
        check_vma=False,
    )
```

```python
import functools

import jax
import jax.numpy as jnp
from jax import lax
from jax.experimental import pallas as pl
from jax.experimental.pallas import tpu as pltpu
from jax.sharding import PartitionSpec as P

MESH = pl.DeviceIdType.MESH
NX, NY, NZ, NC = 4, 4, 16, 8
STEPS, TCAP, SLOTS, BSL, OWN = 16, 16, 16, 4, 4
HA = 2
WINDOW = 2
UNROLL = 64
Z_WAIT, FAR_WAIT = 2, 1


def split_pair(block):
    high = block.astype(jnp.bfloat16)
    low = (block - high.astype(jnp.float32)).astype(jnp.bfloat16)
    return jnp.concatenate([high, low], axis=-1)


def kernel(
    a_ref, b_ref, trip, live, order, out,
    abuf, bbuf, ahl, bhl, cum, sbuf, via, rbuf, prev, lefts, rights, last,
    ss_a, rs_a, ss_x0, rs_x0, ss_k0, rs_k0, ss_z, rs_z, ss_x1, rs_x1, ss_k1, rs_k1, ss_c, rs_c,
):
    row, c, y = lax.axis_index("row"), lax.axis_index("col"), lax.axis_index("depth")
    x, zh, k = row // 4, (row // 2) % 2, row % 2

    def dev(dx=0, dz=0, dk=0, dc=0, dy=0):
        r = ((x + dx + NX) % NX) * 4 + ((zh + dz) % 2) * 2 + (k + dk) % 2
        return (r, c + dc, (y + dy + NY) % NY)

    def copy(src, dst, ss, rs, to):
        return pltpu.make_async_remote_copy(
            src_ref=src, dst_ref=dst, send_sem=ss, recv_sem=rs, device_id=to, device_id_type=MESH
        )

    barrier = pltpu.get_barrier_semaphore()

    def greet(to):
        pl.semaphore_signal(barrier, inc=1, device_id=to, device_id_type=MESH)

    partners = [dev(dx=1), dev(dx=2), dev(dx=3), dev(dk=1), dev(dy=1), dev(dy=-1)]
    for p in partners:
        greet(p)

    @pl.when(c > 0)
    def _():
        greet(dev(dc=-1))

    @pl.when(c < NC - 1)
    def _():
        greet(dev(dc=1))

    ends = (c > 0).astype(jnp.int32) + (c < NC - 1).astype(jnp.int32)
    pl.semaphore_wait(barrier, len(partners) + ends + zh)
    greet(dev(dz=1))

    wa = 4 // HA

    def a_copy(direction, t, h):
        j = c - t * direction
        part = pl.ds(h * wa, wa)
        src = a_ref.at[part] if t == 0 else abuf.at[j, part]
        return copy(
            src, abuf.at[j, part], ss_a.at[(1 - direction) // 2, t, h], rs_a.at[j, h], dev(dc=direction)
        )

    def a_arrived(j, h):
        part = pl.ds(h * wa, wa)
        copy(abuf.at[j, part], abuf.at[j, part], ss_a.at[0, 0, h], rs_a.at[j, h], dev(dc=0, dk=1)).wait_recv()

    def x0_copy(d):
        return copy(b_ref, bbuf.at[0, d, 0], ss_x0.at[d - 1], rs_x0.at[d - 1], dev(dx=-d))

    def k0_copy(d):
        src = b_ref if d == 0 else bbuf.at[0, d, 0]
        return copy(src, bbuf.at[0, d, 1], ss_k0.at[d], rs_k0.at[d], dev(dk=1))

    def z_copy():
        return copy(b_ref, bbuf.at[1, 0, 0], ss_z.at[0], rs_z.at[0], dev(dz=1))

    def x1_copy(d):
        return copy(bbuf.at[1, 0, 0], bbuf.at[1, d, 0], ss_x1.at[d - 1], rs_x1.at[d - 1], dev(dx=-d))

    def k1_copy(d):
        return copy(bbuf.at[1, d, 0], bbuf.at[1, d, 1], ss_k1.at[d], rs_k1.at[d], dev(dk=1))

    def c_copy(side, stage):
        keep = pl.ds(2 * (side if stage == 2 else 1 - side), 2)
        dst = via.at[side] if stage == 0 else rbuf.at[side, keep]
        return copy(
            sbuf.at[side, stage], dst, ss_c.at[side, stage], rs_c.at[side, stage], dev(dy=1 - 2 * side)
        )

    def sends(direction, t):
        if direction == 1:
            return (c - t >= 0) & (c < NC - 1)
        return (c + t <= NC - 1) & (c > 0)

    def send_a(direction, n):
        @pl.when(sends(direction, n // HA))
        def _():
            if n >= WINDOW:
                a_copy(direction, *divmod(n - WINDOW, HA)).wait_send()
            a_copy(direction, *divmod(n, HA)).start()

    def drain_a(direction, n):
        @pl.when(sends(direction, n // HA) & jnp.logical_not(sends(direction, (n + WINDOW) // HA)))
        def _():
            a_copy(direction, *divmod(n, HA)).wait_send()

    for h in range(HA):
        for direction in (1, -1):
            send_a(direction, h)

    @pl.when(zh == 1)
    def _():
        z_copy().start()
    for d in (2, 1, 3):
        x0_copy(d).start()
    k0_copy(0).start()

    def hear_far():
        @pl.when(zh == 0)
        def _():
            pl.semaphore_wait(barrier, 1)
            z_copy().start()

    def step_of(i):
        dz, dx, dk = i // 8, (i // 2) % 4, i % 2
        return ((x + dx) % NX) * 4 + ((zh + dz) % 2) * 2 + (k + dk) % 2

    def chain(i, heads):
        s = step_of(i)
        count = live[s]
        for t in range(TCAP):
            q = trip[2, s, t]
            before = jnp.int32(STEPS * TCAP)
            for n in range(SLOTS):
                before = jnp.where(q == n, heads[n], before)
            prev[i * TCAP + t] = before
            lefts[i * TCAP + t] = trip[0, s, t]
            rights[i * TCAP + t] = i * BSL + trip[1, s, t]
            here = jnp.where(t < count, q, SLOTS)
            heads = tuple(jnp.where(here == n, i * TCAP + t, heads[n]) for n in range(SLOTS))
        return heads

    none = jnp.int32(STEPS * TCAP)
    heads = lax.fori_loop(0, STEPS, chain, (none,) * SLOTS)
    for n in range(SLOTS):
        last[n] = heads[n]
    cum[STEPS * TCAP] = jnp.zeros((128, 128), jnp.float32)

    def split_a(j, src):
        for n in range(4):
            ahl[j * 4 + n] = split_pair(src(n))

    split_a(c, lambda n: a_ref[n])

    def split_b(i, src):
        for n in range(4):
            bhl[i * 4 + n] = split_pair(src(n))

    split_b(0, lambda n: b_ref[n])

    def forward_z():
        z_copy().wait_recv()
        for d in (2, 1, 3):
            x1_copy(d).start()
        k1_copy(0).start()
        split_b(8, lambda n: bbuf[1, 0, 0, n])

    def forward_x0(d):
        x0_copy(d).wait_recv()
        k0_copy(d).start()
        split_b(d * 2, lambda n: bbuf[0, d, 0, n])

    def forward_x1(d):
        x1_copy(d).wait_recv()
        k1_copy(d).start()
        split_b(8 + d * 2, lambda n: bbuf[1, d, 0, n])

    def take_k0(d):
        k0_copy(d).wait_recv()
        split_b(d * 2 + 1, lambda n: bbuf[0, d, 1, n])

    def take_k1(d):
        k1_copy(d).wait_recv()
        split_b(8 + d * 2 + 1, lambda n: bbuf[1, d, 1, n])

    jobs = {t: [] for t in range(NC + 3)}
    jobs[Z_WAIT].append(forward_z)
    for n, d in enumerate((1, 3, 2)):
        jobs[1 + n].append(functools.partial(forward_x0, d))
        jobs[Z_WAIT + 3 + n].append(functools.partial(forward_x1, d))
    for n, d in enumerate((0, 1, 3, 2)):
        jobs[4 + n].append(functools.partial(take_k0, d))
        jobs[Z_WAIT + 4 + n].append(functools.partial(take_k1, d))

    for t in range(1, NC):
        if t == NC - 1:
            for later in range(t, NC + 3):
                for job in jobs[later]:
                    job()
        for h in range(HA):
            for direction in (1, -1):
                @pl.when((c - t * direction >= 0) & (c - t * direction <= NC - 1))
                def _():
                    a_arrived(c - t * direction, h)

                send_a(direction, t * HA + h)

        @pl.when(c - t >= 0)
        def _():
            split_a(c - t, lambda n: abuf[c - t, n])

        @pl.when(c + t <= NC - 1)
        def _():
            split_a(c + t, lambda n: abuf[c + t, n])

        if t == FAR_WAIT:
            hear_far()
        if t < NC - 1:
            for job in jobs[t]:
                job()

    def product(i, carry):
        right = bhl[rights[i]]
        both = jnp.dot(
            ahl[lefts[i]], jnp.concatenate([right, right], axis=0), preferred_element_type=jnp.float32
        )
        cum[i] = cum[prev[i]] + (both[:, :128] + both[:, 128:])
        return carry

    lax.fori_loop(0, STEPS * TCAP, product, 0, unroll=UNROLL)

    def total(owner, n):
        return cum[last[order[((y + owner + NY) % NY) * OWN + n]]]

    for stage in (0, 1):
        for side in (0, 1):
            for n in range(2):
                if stage == 0:
                    sbuf[side, 0, n] = total(2, 2 * side + n)
                else:
                    sbuf[side, 1, n] = total(1 - 2 * side, 2 * (1 - side) + n)
            c_copy(side, stage).start()
    for side in (0, 1):
        for n in range(2):
            sbuf[side, 2, n] = total(1 - 2 * side, 2 * side + n)
    for n in range(OWN):
        out[n] = total(0, n)
    for side in (0, 1):
        c_copy(side, 0).wait_recv()
        sbuf[side, 2] += via[side]
        c_copy(side, 2).start()
    for stage in (1, 2):
        for side in (0, 1):
            c_copy(side, stage).wait_recv()
            keep = pl.ds(2 * (side if stage == 2 else 1 - side), 2)
            out[keep] += rbuf[side, keep]

    for n in range(NC * HA):
        drain_a(1, n)
        drain_a(-1, n)
    z_copy().wait_send()
    for d in range(1, 4):
        x0_copy(d).wait_send()
        x1_copy(d).wait_send()
    for d in range(4):
        k0_copy(d).wait_send()
        k1_copy(d).wait_send()
    for side in (0, 1):
        for stage in range(3):
            c_copy(side, stage).wait_send()


def on_device(a_blocks, b_blocks, triples, live, c_order):
    f32, bf16 = jnp.float32, jnp.bfloat16
    vmem, smem = pl.BlockSpec(memory_space=pltpu.VMEM), pl.BlockSpec(memory_space=pltpu.SMEM)
    dma = pltpu.SemaphoreType.DMA
    result = pl.pallas_call(
        kernel,
        out_shape=jax.ShapeDtypeStruct((OWN, 128, 128), f32),
        in_specs=[vmem, vmem, smem, smem, smem],
        out_specs=vmem,
        scratch_shapes=[
            pltpu.VMEM((NC, 4, 128, 128), f32),
            pltpu.VMEM((2, 4, 2, 4, 128, 128), f32),
            pltpu.VMEM((NC * 4, 128, 256), bf16),
            pltpu.VMEM((STEPS * 4, 128, 256), bf16),
            pltpu.VMEM((STEPS * TCAP + 1, 128, 128), f32),
            pltpu.VMEM((2, 3, 2, 128, 128), f32),
            pltpu.VMEM((2, 2, 128, 128), f32),
            pltpu.VMEM((2, OWN, 128, 128), f32),
            pltpu.SMEM((STEPS * TCAP,), jnp.int32),
            pltpu.SMEM((STEPS * TCAP,), jnp.int32),
            pltpu.SMEM((STEPS * TCAP,), jnp.int32),
            pltpu.SMEM((SLOTS,), jnp.int32),
            dma((2, NC, HA)), dma((NC, HA)),
            dma((3,)), dma((3,)), dma((4,)), dma((4,)),
            dma((1,)), dma((1,)), dma((3,)), dma((3,)), dma((4,)), dma((4,)),
            dma((2, 3)), dma((2, 3)),
        ],
        compiler_params=pltpu.CompilerParams(
            collective_id=0, has_side_effects=True, vmem_limit_bytes=56 * 1024 * 1024
        ),
        name="block_sparse_product",
    )(a_blocks[0, 0, 0], b_blocks[0, 0, 0], jnp.transpose(triples[0, 0, 0], (2, 0, 1)), live[0, 0, 0], c_order[0, 0])
    return result.reshape(1, 1, 1, OWN, 128, 128)


def solution(mesh):
    placed = (
        P("row", "col", "depth", None, None, None),
        P("row", "col", "depth", None, None, None),
        P("row", "col", "depth", None, None, None),
        P("row", "col", "depth", None),
        P("row", "col", None),
    )
    return jax.shard_map(
        on_device,
        mesh=mesh,
        in_specs=placed,
        out_specs=P("row", "col", "depth", None, None, None),
        check_vma=False,
    )
```
